256 devices in a mesh: row: 16 (over x_hi, y, core), col: 16 (over x_lo, z).
Axes of the slice: x: 4 (x_hi: 2, x_lo: 2; x = x_hi * 2 + x_lo), y: 4, z: 8, core: 2. Of those that a mesh axis runs over, the one named last changes fastest.
Arguments:
- shear_stress: float32 [512, 32768], P(None, ('row', 'col')), may hold values from -3.5 to 3.5
- state_var: float32 [512, 32768], P(None, ('row', 'col')), may hold values from -0.4 to 0.4
- a_param: float32 [32768], P(('row', 'col')), may hold values from 0.7 to 1.4
- rate_param: float32 [32768], P(('row', 'col')), may hold values from 0.1 to 0.5
- loading: float32 [32768], P(('row', 'col')), may hold values from 0.1 to 1
- dense_tiles: bfloat16 [32768, 32768], P('row', 'col'), may hold values from -0.03125 to 0.03125
- left_factor: bfloat16 [1024, 32768], P('col', 'row'), may hold values from -0.75 to 0.75
- right_factor: bfloat16 [1024, 32768], P('row', 'col'), may hold values from -0.03125 to 0.03125
- admissible: int32 [16, 16], replicated, may hold values from 0 to 1, as said below
- tile_ranks: int32 [16, 16], replicated, may hold values from 16 to 64
Outputs:
- shear_next: float32 [512, 32768], P(None, ('row', 'col'))
- state_next: float32 [512, 32768], P(None, ('row', 'col'))
The draws below stay inside these ranges and needn't reach their ends.
Inputs may be any that keep to these rules, and one draw needn't show every extreme that they name: `admissible`: tiles on the diagonal and next to it are always dense; elsewhere a tile is dense or low-rank at random.
All inputs are finite; a program needn't handle non-finite values.
Results may differ from the reference program's by a relative error of at most 0.0024.
Values may be sent and summed in bfloat16 or wider, within the bound.
No kernel may reach another device: no remote copies, remote signals or barrier semaphores. Data moves between devices by JAX's collectives and lax.ppermute only.
A program may use at most 64 MiB of HBM per device.

```python
import math
import jax
import jax.numpy as jnp
from jax import lax

TILE = 2048
RANK = 64
SCEN = 512
NB = 16
N = 32768


def draw_admissible(key, part):
    index_line = jnp.arange(NB, dtype=jnp.int32)
    nearby = jnp.abs(index_line[:, None] - index_line[None, :]) <= 1
    coins = jax.random.randint(key, (NB, NB), 0, 4) == 0
    return jnp.where(nearby | coins, 1, 0).astype(jnp.int32)


def touch_ends(array, key, smallest, largest):
    shape = array.shape
    index_at = [jax.random.randint(jax.random.fold_in(key, axis), (), 0, shape[axis]) for axis in range(len(shape))]
    array = array.at[tuple(index_at)].set(smallest)
    longest = shape.index(max(shape))
    index_at[longest] = (index_at[longest] + 1) % shape[longest]
    return array.at[tuple(index_at)].set(largest)


def steps_of(stream_key, dims, split, low, high):
    gain, own = 1.0, jax.random.fold_in(stream_key, 6)
    for position, blocks in split:
        heights = jnp.exp(jax.random.uniform(jax.random.fold_in(own, position), (blocks,), jnp.float32, low / len(split), high / len(split)))
        gain = gain * jnp.repeat(heights, dims[position] // blocks).reshape([-1 if axis == position else 1 for axis in range(len(dims))])
    return gain


def normal_values(key, extent, scale, bound, pieces=(), kind=jnp.bfloat16):
    array = scale * jax.random.normal(key, extent, jnp.float32)
    if pieces:
        array = array * steps_of(key, extent, pieces, -0.22, 0.18)
    return jnp.clip(array, -bound, bound).astype(kind)


def setup_inputs(seed: int = 0) -> dict:
    key_of = jax.random.split(jax.random.key(seed), 11)
    shear_stress = normal_values(key_of[0], (SCEN, N), 0.4, 3.5, ((1, 256),), jnp.float32)
    state_var = jnp.clip(jax.random.uniform(key_of[1], (SCEN, N), jnp.float32, -0.4, 0.4) * steps_of(key_of[1], (SCEN, N), ((1, 256),), -0.4, 0.0), -0.4, 0.4)
    a_param = jnp.clip(jnp.exp(math.log(1.4) - 0.6931472 * jax.random.uniform(key_of[2], (N,), jnp.float32) ** steps_of(key_of[2], (N,), ((0, 256),), -0.2, 0.2)), 0.7, 1.4)
    rate_param = jnp.clip(jnp.exp(math.log(0.5) - 1.609438 * jax.random.uniform(key_of[3], (N,), jnp.float32) ** steps_of(key_of[3], (N,), ((0, 256),), -0.2, 0.2)), 0.1, 0.5)
    loading = jnp.clip(jnp.exp(math.log(1.0) - 2.3025851 * jax.random.uniform(key_of[4], (N,), jnp.float32) ** steps_of(key_of[4], (N,), ((0, 256),), -0.2, 0.2)), 0.1, 1.0)
    dense_tiles = normal_values(key_of[5], (N, N), N ** -0.5, 0.03125, ((0, 16), (1, 16)))
    left_factor = normal_values(key_of[6], (NB * RANK, N), RANK ** -0.5, 0.75, ((0, 16), (1, 16)))
    right_factor = normal_values(key_of[7], (NB * RANK, N), N ** -0.5, 0.03125, ((0, 16), (1, 16)))
    admissible = draw_admissible(jax.random.fold_in(key_of[10], 71), 0)
    tile_ranks = touch_ends(jax.random.randint(key_of[9], (NB, NB), RANK // 4, RANK + 1), jax.random.fold_in(key_of[9], 1), RANK // 4, RANK).astype(jnp.int32)
    return dict(shear_stress=shear_stress, state_var=state_var, a_param=a_param, rate_param=rate_param, loading=loading, dense_tiles=dense_tiles, left_factor=left_factor, right_factor=right_factor, admissible=admissible, tile_ranks=tile_ranks)


def slip_velocity(shear_now, state_now, a_param):
    return jnp.sinh(shear_now / a_param[None, :]) * jnp.exp(-state_now)


def tile_product(vec_tile, dense_tile, left_tile, right_tile, is_dense, rank_here):
    def dense_branch(operands):
        return lax.dot_general(operands[0], operands[1], (((1,), (1,)), ((), ())), preferred_element_type=jnp.float32)

    def factor_branch(operands):
        projection = lax.dot_general(operands[0], operands[3], (((1,), (1,)), ((), ())), preferred_element_type=jnp.float32)
        keep_mask = jnp.arange(projection.shape[1], dtype=jnp.int32)[None, :] < rank_here
        projection = jnp.where(keep_mask, projection, jnp.zeros_like(projection)).astype(jnp.bfloat16)
        return jnp.dot(projection, operands[2], preferred_element_type=jnp.float32)

    return lax.cond(is_dense == 1, dense_branch, factor_branch, (vec_tile, dense_tile, left_tile, right_tile))


def interaction(rounded, dense_tiles, left_factor, right_factor, admissible, tile_ranks):
    def target_row(row_tile):
        def source_col(accum_sum, col_tile):
            vec_tile = lax.dynamic_slice_in_dim(rounded, col_tile * TILE, TILE, 1)
            dense_tile = lax.dynamic_slice(dense_tiles, (row_tile * TILE, col_tile * TILE), (TILE, TILE))
            left_tile = lax.dynamic_slice(left_factor, (col_tile * RANK, row_tile * TILE), (RANK, TILE))
            right_tile = lax.dynamic_slice(right_factor, (row_tile * RANK, col_tile * TILE), (RANK, TILE))
            term = tile_product(vec_tile, dense_tile, left_tile, right_tile, admissible[row_tile, col_tile], tile_ranks[row_tile, col_tile])
            return accum_sum + term, None

        accum_sum, unused_out = lax.scan(source_col, jnp.zeros((SCEN, TILE), jnp.float32), jnp.arange(NB, dtype=jnp.int32))
        return accum_sum

    blocks = lax.map(target_row, jnp.arange(NB, dtype=jnp.int32))
    return jnp.transpose(blocks, (1, 0, 2)).reshape(SCEN, N)


def reference(shear_stress, state_var, a_param, rate_param, loading, dense_tiles, left_factor, right_factor, admissible, tile_ranks):
    def rates(shear_now, state_now):
        velocity = slip_velocity(shear_now, state_now, a_param)
        rounded = velocity.astype(jnp.bfloat16)
        pushed = interaction(rounded, dense_tiles, left_factor, right_factor, admissible, tile_ranks)
        k_shear = loading[None, :] - pushed
        k_state = rate_param[None, :] * (jnp.exp(-state_now) - jnp.abs(velocity))
        return k_shear, k_state

    k_shear1, k_state1 = rates(shear_stress, state_var)
    shear_mid = shear_stress + 0.5 * k_shear1
    state_mid = state_var + 0.5 * k_state1
    k_shear2, k_state2 = rates(shear_mid, state_mid)
    shear_next = shear_stress + 0.25 * (k_shear1 + k_shear2)
    state_next = state_var + 0.25 * (k_state1 + k_state2)
    return (shear_next, state_next)
```

```python
import functools

import jax
import jax.numpy as jnp
from jax import lax
from jax.experimental import pallas as pl
from jax.experimental.pallas import tpu as pltpu
from jax.sharding import Mesh
from jax.sharding import PartitionSpec as P

AXES = ("xh", "y", "k", "xl", "z")
ROW = ("xh", "y", "k")
COL = ("xl", "z")
PIECE = 128
STEPS = ((4,), (3, 5), (2, 6), (1, 7, 0))
Y_STEPS = (0, 3, 1, 2)
VMEM_BYTES = 24 * 2**20
FAR_VMEM_BYTES = 46 * 2**20
F32 = jnp.float32
BF16 = jnp.bfloat16


def column_pairs():
    pairs = []
    for source in range(256):
        xh, y, k, xl, z = source >> 7, (source >> 5) & 3, (source >> 4) & 1, (source >> 3) & 1, source & 7
        ahead = (z - 2 * y - k) & 7
        k2 = (ahead + 1) & 1
        y2 = (y + (3 + k2 - ahead) // 2) & 3
        pairs.append((source, (((xl * 4 + y2) * 2 + k2) * 2 + xh) * 8 + 2 * y + k))
    return pairs


def piece_at(xh, y, k, z):
    return xh * 8 + ((z + 3 - 2 * (y - (z >> 1)) + k) & 7)


def ring(n, step):
    return [(i, (i + step) % n) for i in range(n)]


def gather_sources(piece, aside):
    moved = lax.ppermute(piece, AXES, column_pairs())
    moved, aside = lax.optimization_barrier((moved, aside))
    got = []
    for array in (moved, lax.ppermute(moved, "xh", ring(2, 1))):
        above = lax.ppermute(array, "y", ring(4, 1))
        below = lax.ppermute(array, "y", ring(4, 3))
        far = lax.ppermute(array, "y", ring(4, 2))
        got += [array, above, below, far]
    return got + [lax.ppermute(array, "k", ring(2, 1)) for array in got], aside


def dot_nt(a, b):
    return lax.dot_general(a, b, (((1,), (1,)), ((), ())), preferred_element_type=F32)


def tile_term(here, at, x_ref, d_hbm, lr_ref, proj_ref, own_ref, other_ref, d_ref, sems):
    width = x_ref.shape[1]
    places = [(here[3] + step) & 7 for step in at]
    sides = (here[6], 1 - here[6])

    def fetch(i, side):
        source = d_hbm.at[sides[side], places[i]]
        return pltpu.make_async_copy(source, d_ref.at[i, side], sems.at[i, side])

    def put(i, value):
        own_ref[i] = value[:, :PIECE]
        other_ref[i] = value[:, PIECE:].astype(BF16)

    @pl.when(here[4] == 1)
    def _():
        for i in range(len(at)):
            for side in range(2):
                fetch(i, side).start()
        for i in range(len(at)):
            for side in range(2):
                fetch(i, side).wait()
            put(i, dot_nt(x_ref[...], d_ref[i].reshape(2 * PIECE, width)))

    @pl.when(here[4] != 1)
    def _():
        rank = lr_ref.shape[0] // 2
        for i in range(len(at)):
            starts = [pl.multiple_of((side * 8 + places[i]) * PIECE, PIECE) for side in sides]
            left = [lr_ref[:rank, pl.ds(start, PIECE)] for start in starts]
            left = jnp.concatenate(left, axis=1)
            put(i, jnp.dot(proj_ref[...], left, preferred_element_type=F32))


def first_kernel(at, here, *refs):
    pieces = refs[:16]
    d_hbm, lr_ref, own_ref, other_ref, x_ref, proj_ref, d_ref, sems = refs[16:]
    for i in range(16):
        dk, dx, dy = i // 8, i // 4 % 2, Y_STEPS[i % 4]
        place = piece_at((here[0] + dx) & 1, (here[1] + dy) & 3, (here[2] + dk) & 1, here[3])
        x_ref[:, pl.ds(pl.multiple_of(place * PIECE, PIECE), PIECE)] = pieces[i][...]

    @pl.when(here[4] != 1)
    def _():
        rank = lr_ref.shape[0] // 2
        proj = dot_nt(x_ref[...], lr_ref[rank:, :])
        keep = lax.broadcasted_iota(jnp.int32, proj.shape, 1) < here[5]
        proj_ref[...] = jnp.where(keep, proj, 0.0).astype(BF16)

    tile_term(here, at, x_ref, d_hbm, lr_ref, proj_ref, own_ref, other_ref, d_ref, sems)


def later_kernel(at, here, x_ref, proj_ref, d_hbm, lr_ref, own_ref, other_ref, d_ref, sems):
    tile_term(here, at, x_ref, d_hbm, lr_ref, proj_ref, own_ref, other_ref, d_ref, sems)


def tile_terms(here, pieces, dense4, factors):
    scen = pieces[0].shape[0]
    width, rank = dense4.shape[3], factors.shape[0] // 2
    scalars = pl.BlockSpec(memory_space=pltpu.SMEM)
    near = pl.BlockSpec(memory_space=pltpu.VMEM)
    distant = pl.BlockSpec(memory_space=pltpu.HBM)

    def call(kernel, at, in_specs, more, name, vmem_bytes):
        out_shape = [
            jax.ShapeDtypeStruct((len(at), scen, PIECE), F32),
            jax.ShapeDtypeStruct((len(at), scen, PIECE), BF16),
        ] + more
        return pl.pallas_call(
            functools.partial(kernel, at),
            in_specs=in_specs,
            out_specs=[near] * len(out_shape),
            out_shape=out_shape,
            scratch_shapes=[
                pltpu.VMEM((len(at), 2, PIECE, width), BF16),
                pltpu.SemaphoreType.DMA((len(at), 2)),
            ],
            compiler_params=pltpu.CompilerParams(vmem_limit_bytes=vmem_bytes),
            cost_estimate=pl.CostEstimate(
                flops=2 * scen * width * 2 * PIECE * len(at),
                bytes_accessed=len(at) * 2**20,
                transcendentals=0,
            ),
            name=name,
        )

    *terms, x, proj = call(
        first_kernel,
        STEPS[0],
        [scalars] + [near] * 16 + [distant, near],
        [
            jax.ShapeDtypeStruct((scen, width), BF16),
            jax.ShapeDtypeStruct((scen, rank), BF16),
        ],
        "first_terms",
        FAR_VMEM_BYTES,
    )(here, *pieces, dense4, factors)
    terms = [terms]
    for at in STEPS[1:]:
        in_specs = [scalars, near, near, distant, near]
        terms.append(
            call(later_kernel, at, in_specs, [], "later_terms", VMEM_BYTES)(
                here, x, proj, dense4, factors
            )
        )
    return terms


def summed(terms):
    both = {}
    for at, (own, other) in zip(STEPS, terms):
        got = lax.ppermute(other, "xl", ring(2, 1)).astype(F32)
        for i, step in enumerate(at):
            both[step] = own[i] + got[i]
    far = both[4].astype(BF16)
    half = far.shape[0] // 2
    none = jnp.zeros_like(far[:half], dtype=F32)
    up = lax.ppermute(far[:half], "z", ring(8, 1))
    down = lax.ppermute(far[half:], "z", ring(8, 7))
    up = jnp.concatenate([up.astype(F32), none], axis=0)
    down = jnp.concatenate([none, down.astype(F32)], axis=0)
    for step in (3, 2, 1):
        up = lax.ppermute((up + both[step]).astype(BF16), "z", ring(8, 1)).astype(F32)
        down = lax.ppermute((down + both[8 - step]).astype(BF16), "z", ring(8, 7)).astype(F32)
    return both[0] + down + up


def on_device(
    shear_stress,
    state_var,
    a_param,
    rate_param,
    loading,
    dense_tiles,
    left_factor,
    right_factor,
    admissible,
    tile_ranks,
):
    row, col = lax.axis_index(ROW), lax.axis_index(COL)
    xh, y, k = (lax.axis_index(a) for a in ROW)
    xl, z = (lax.axis_index(a) for a in COL)
    here = jnp.stack([xh, y, k, z, admissible[row, col], tile_ranks[row, col], xl])
    here = here.astype(jnp.int32)

    def rates(shear_now, state_now, aside):
        grown = jnp.exp(-state_now)
        velocity = jnp.sinh(shear_now / a_param[None, :]) * grown
        pieces, aside = gather_sources(velocity.astype(BF16), aside)
        here, factors = aside
        pushed = summed(tile_terms(here, pieces, dense4, factors))
        k_shear = loading[None, :] - pushed
        k_state = rate_param[None, :] * (grown - jnp.abs(velocity))
        return k_shear, k_state, aside

    dense4 = dense_tiles.reshape(2, 8, PIECE, dense_tiles.shape[1])
    aside = here, jnp.concatenate([left_factor, right_factor], axis=0)
    k_shear1, k_state1, aside = rates(shear_stress, state_var, aside)
    k_shear2, k_state2, _ = rates(
        shear_stress + 0.5 * k_shear1, state_var + 0.5 * k_state1, aside
    )
    shear_next = shear_stress + 0.25 * (k_shear1 + k_shear2)
    state_next = state_var + 0.25 * (k_state1 + k_state2)
    return shear_next, state_next


def solution(mesh):
    torus = Mesh(mesh.devices.reshape(2, 4, 2, 2, 8), AXES)
    both = ROW + COL
    in_specs = (
        P(None, both),
        P(None, both),
        P(both),
        P(both),
        P(both),
        P(ROW, COL),
        P(COL, ROW),
        P(ROW, COL),
        P(),
        P(),
    )
    out_specs = (P(None, both), P(None, both))
    return jax.shard_map(
        on_device, mesh=torus, in_specs=in_specs, out_specs=out_specs, check_vma=False
    )
```

```python
import functools

import jax
import jax.numpy as jnp
from jax import lax
from jax.experimental import pallas as pl
from jax.experimental.pallas import tpu as pltpu
from jax.sharding import Mesh
from jax.sharding import PartitionSpec as P

AXES = ("xh", "y", "k", "xl", "z")
ROW = ("xh", "y", "k")
COL = ("xl", "z")
PIECE = 128
STEPS = ((4,), (3, 5), (2, 6), (1, 7, 0))
Y_STEPS = (0, 3, 1, 2)
VMEM_BYTES = 24 * 2**20
FAR_VMEM_BYTES = 46 * 2**20
F32 = jnp.float32
BF16 = jnp.bfloat16


def column_pairs():
    pairs = []
    for source in range(256):
        xh, y, k, xl, z = source >> 7, (source >> 5) & 3, (source >> 4) & 1, (source >> 3) & 1, source & 7
        ahead = (z - 2 * y - k) & 7
        k2 = (ahead + 1) & 1
        y2 = (y + (3 + k2 - ahead) // 2) & 3
        pairs.append((source, (((xl * 4 + y2) * 2 + k2) * 2 + xh) * 8 + 2 * y + k))
    return pairs


def piece_at(xh, y, k, z):
    return xh * 8 + ((z + 3 - 2 * (y - (z >> 1)) + k) & 7)


def ring(n, step):
    return [(i, (i + step) % n) for i in range(n)]


def gather_sources(piece, aside):
    moved = lax.ppermute(piece, AXES, column_pairs())
    moved, aside = lax.optimization_barrier((moved, aside))
    across = lax.ppermute(moved, "xh", ring(2, 1))
    far = lax.ppermute(moved, "y", ring(4, 2))
    got = []
    for array, opposite in ((moved, far), (across, lax.ppermute(far, "xh", ring(2, 1)))):
        above = lax.ppermute(array, "y", ring(4, 1))
        below = lax.ppermute(array, "y", ring(4, 3))
        got += [array, above, below, opposite]
    return got + [lax.ppermute(array, "k", ring(2, 1)) for array in got], aside


def dot_nt(a, b):
    return lax.dot_general(a, b, (((1,), (1,)), ((), ())), preferred_element_type=F32)


def tile_term(here, at, x_ref, d_hbm, lr_ref, proj_ref, own_ref, other_ref, d_ref, sems):
    width = x_ref.shape[1]
    places = [(here[3] + step) & 7 for step in at]
    sides = (here[6], 1 - here[6])

    def fetch(i, side):
        source = d_hbm.at[sides[side], places[i]]
        return pltpu.make_async_copy(source, d_ref.at[i, side], sems.at[i, side])

    def put(i, value):
        own_ref[i] = value[:, :PIECE]
        other_ref[i] = value[:, PIECE:].astype(BF16)

    @pl.when(here[4] == 1)
    def _():
        for i in range(len(at)):
            for side in range(2):
                fetch(i, side).start()
        for i in range(len(at)):
            for side in range(2):
                fetch(i, side).wait()
            put(i, dot_nt(x_ref[...], d_ref[i].reshape(2 * PIECE, width)))

    @pl.when(here[4] != 1)
    def _():
        rank = lr_ref.shape[0] // 2
        for i in range(len(at)):
            starts = [pl.multiple_of((side * 8 + places[i]) * PIECE, PIECE) for side in sides]
            left = [lr_ref[:rank, pl.ds(start, PIECE)] for start in starts]
            left = jnp.concatenate(left, axis=1)
            put(i, jnp.dot(proj_ref[...], left, preferred_element_type=F32))


def first_kernel(at, here, *refs):
    pieces = refs[:16]
    d_hbm, lr_ref, own_ref, other_ref, x_ref, proj_ref, d_ref, sems = refs[16:]
    for i in range(16):
        dk, dx, dy = i // 8, i // 4 % 2, Y_STEPS[i % 4]
        place = piece_at((here[0] + dx) & 1, (here[1] + dy) & 3, (here[2] + dk) & 1, here[3])
        x_ref[:, pl.ds(pl.multiple_of(place * PIECE, PIECE), PIECE)] = pieces[i][...]

    @pl.when(here[4] != 1)
    def _():
        rank = lr_ref.shape[0] // 2
        proj = dot_nt(x_ref[...], lr_ref[rank:, :])
        keep = lax.broadcasted_iota(jnp.int32, proj.shape, 1) < here[5]
        proj_ref[...] = jnp.where(keep, proj, 0.0).astype(BF16)

    tile_term(here, at, x_ref, d_hbm, lr_ref, proj_ref, own_ref, other_ref, d_ref, sems)


def later_kernel(at, here, x_ref, proj_ref, d_hbm, lr_ref, own_ref, other_ref, d_ref, sems):
    tile_term(here, at, x_ref, d_hbm, lr_ref, proj_ref, own_ref, other_ref, d_ref, sems)


def tile_terms(here, pieces, dense4, factors):
    scen = pieces[0].shape[0]
    width, rank = dense4.shape[3], factors.shape[0] // 2
    scalars = pl.BlockSpec(memory_space=pltpu.SMEM)
    near = pl.BlockSpec(memory_space=pltpu.VMEM)
    distant = pl.BlockSpec(memory_space=pltpu.HBM)

    def call(kernel, at, in_specs, more, name, vmem_bytes):
        out_shape = [
            jax.ShapeDtypeStruct((len(at), scen, PIECE), F32),
            jax.ShapeDtypeStruct((len(at), scen, PIECE), BF16),
        ] + more
        return pl.pallas_call(
            functools.partial(kernel, at),
            in_specs=in_specs,
            out_specs=[near] * len(out_shape),
            out_shape=out_shape,
            scratch_shapes=[
                pltpu.VMEM((len(at), 2, PIECE, width), BF16),
                pltpu.SemaphoreType.DMA((len(at), 2)),
            ],
            compiler_params=pltpu.CompilerParams(vmem_limit_bytes=vmem_bytes),
            cost_estimate=pl.CostEstimate(
                flops=2 * scen * width * 2 * PIECE * len(at),
                bytes_accessed=len(at) * 2**20,
                transcendentals=0,
            ),
            name=name,
        )

    *terms, x, proj = call(
        first_kernel,
        STEPS[0],
        [scalars] + [near] * 16 + [distant, near],
        [
            jax.ShapeDtypeStruct((scen, width), BF16),
            jax.ShapeDtypeStruct((scen, rank), BF16),
        ],
        "first_terms",
        FAR_VMEM_BYTES,
    )(here, *pieces, dense4, factors)
    terms = [terms]
    for at in STEPS[1:]:
        in_specs = [scalars, near, near, distant, near]
        terms.append(
            call(later_kernel, at, in_specs, [], "later_terms", VMEM_BYTES)(
                here, x, proj, dense4, factors
            )
        )
    return terms


def summed(terms):
    both = {}
    for at, (own, other) in zip(STEPS, terms):
        got = lax.ppermute(other, "xl", ring(2, 1)).astype(F32)
        for i, step in enumerate(at):
            both[step] = own[i] + got[i]
    up = lax.ppermute(both[4].astype(BF16), "z", ring(8, 1)).astype(F32)
    down = 0.0
    for step in (3, 2, 1):
        up = lax.ppermute((up + both[step]).astype(BF16), "z", ring(8, 1)).astype(F32)
        down = lax.ppermute((down + both[8 - step]).astype(BF16), "z", ring(8, 7)).astype(F32)
    return both[0] + down + up


def on_device(
    shear_stress,
    state_var,
    a_param,
    rate_param,
    loading,
    dense_tiles,
    left_factor,
    right_factor,
    admissible,
    tile_ranks,
):
    row, col = lax.axis_index(ROW), lax.axis_index(COL)
    xh, y, k = (lax.axis_index(a) for a in ROW)
    xl, z = (lax.axis_index(a) for a in COL)
    here = jnp.stack([xh, y, k, z, admissible[row, col], tile_ranks[row, col], xl])
    here = here.astype(jnp.int32)

    def rates(shear_now, state_now, aside):
        grown = jnp.exp(-state_now)
        velocity = jnp.sinh(shear_now / a_param[None, :]) * grown
        pieces, aside = gather_sources(velocity.astype(BF16), aside)
        here, factors = aside
        pushed = summed(tile_terms(here, pieces, dense4, factors))
        k_shear = loading[None, :] - pushed
        k_state = rate_param[None, :] * (grown - jnp.abs(velocity))
        return k_shear, k_state, aside

    dense4 = dense_tiles.reshape(2, 8, PIECE, dense_tiles.shape[1])
    aside = here, jnp.concatenate([left_factor, right_factor], axis=0)
    k_shear1, k_state1, aside = rates(shear_stress, state_var, aside)
    k_shear2, k_state2, _ = rates(
        shear_stress + 0.5 * k_shear1, state_var + 0.5 * k_state1, aside
    )
    shear_next = shear_stress + 0.25 * (k_shear1 + k_shear2)
    state_next = state_var + 0.25 * (k_state1 + k_state2)
    return shear_next, state_next


def solution(mesh):
    torus = Mesh(mesh.devices.reshape(2, 4, 2, 2, 8), AXES)
    both = ROW + COL
    in_specs = (
        P(None, both),
        P(None, both),
        P(both),
        P(both),
        P(both),
        P(ROW, COL),
        P(COL, ROW),
        P(ROW, COL),
        P(),
        P(),
    )
    out_specs = (P(None, both), P(None, both))
    return jax.shard_map(
        on_device, mesh=torus, in_specs=in_specs, out_specs=out_specs, check_vma=False
    )
```
